128 devices in a mesh: fsdp: 16 (over z_hi, x, core), tp: 8 (over z_lo, y).
Axes of the slice: x: 4, y: 4, z: 4 (z_hi: 2, z_lo: 2; z = z_hi * 2 + z_lo), core: 2. Of those that a mesh axis runs over, the one named last changes fastest.
Arguments:
- master: float32 [4096, 15360], P(('fsdp', 'tp')), may hold values from -0.09375 to 0.09375
- queries: bfloat16 [128, 8, 4096], P('fsdp', None, 'tp'), may hold values from -100 to 100
- new_token_key_value: bfloat16 [128, 8, 2, 1024], P('fsdp', None, None, 'tp'), may hold values from -6 to 6
- out_weight: bfloat16 [4096, 4096], P('tp'), may hold values from -0.09375 to 0.09375
- kv_cache: bfloat16 [128, 2, 8, 1024, 128], P('fsdp', None, 'tp'), may hold values from -8 to 8
- lengths: int32 [128], P('fsdp'), may hold values from 2 to 1024
Outputs:
- new_weight: bfloat16 [4096, 15360], P(None, 'tp')
- attn_out: bfloat16 [128, 8, 4096], P('fsdp', None, 'tp')
The draws below stay inside these ranges and needn't reach their ends.
All inputs are finite; a program needn't handle non-finite values.
Results may differ from the reference program's by a relative error of at most 0.0057.
Values may be sent and summed in bfloat16 or wider, within the bound.
No kernel may reach another device: no remote copies, remote signals or barrier semaphores. Data moves between devices by JAX's collectives and lax.ppermute only.
A program may use at most 128 MiB of HBM per device.

```python
import math
import jax
import jax.numpy as jnp
from jax import lax

D = 4096
FFW = 15360
QUERY_HEAD_COUNT = 32
KEY_VALUE_HEADS = 8
HEAD_SIZE = 128
DECODE_STEPS = 8
CACHE_LENGTH = 1024
DECODE_ROWS = 128


def anchor_keys(key):
    return jnp.clip(jax.random.normal(key, (DECODE_ROWS, KEY_VALUE_HEADS, HEAD_SIZE), jnp.float32), -4.0, 4.0)


def draw_queries(key, part):
    key = jax.random.fold_in(key, 2)
    leading_part = jax.random.fold_in(key, 0)
    values = jnp.clip(2.0 * jax.random.normal(leading_part, (DECODE_ROWS, DECODE_STEPS, QUERY_HEAD_COUNT, HEAD_SIZE), jnp.float32), -8.0, 8.0)
    return values.reshape(DECODE_ROWS, DECODE_STEPS, QUERY_HEAD_COUNT * HEAD_SIZE).astype(jnp.bfloat16)


def draw_kv_cache(key, part):
    leading = anchor_keys(key)
    key = jax.random.fold_in(key, 1)
    leading_part, trailing_part = jax.random.split(key)
    key_portion = jnp.clip(jax.random.normal(leading_part, (DECODE_ROWS, KEY_VALUE_HEADS, CACHE_LENGTH, HEAD_SIZE), jnp.float32), -4.0, 4.0)
    value_portion = jnp.clip(2.0 * jax.random.normal(trailing_part, (DECODE_ROWS, KEY_VALUE_HEADS, CACHE_LENGTH, HEAD_SIZE), jnp.float32), -8.0, 8.0)
    key_portion = key_portion.at[:, :, 0, :].set(leading)
    return jnp.stack([key_portion, value_portion], axis=1).astype(jnp.bfloat16)


def draw_lengths(key, part):
    key = jax.random.fold_in(key, 3)
    leading_part, trailing_part = jax.random.split(key)
    highest = int(math.log2(CACHE_LENGTH))
    exponent = jax.random.randint(leading_part, (DECODE_ROWS,), 1, highest)
    base_len = jnp.left_shift(jnp.ones((DECODE_ROWS,), jnp.int32), exponent)
    extra_len = jax.random.randint(trailing_part, (DECODE_ROWS,), 0, base_len)
    result = (base_len + extra_len).astype(jnp.int32)
    result = result.at[0].set(CACHE_LENGTH)
    result = result.at[1].set(2)
    return result.astype(jnp.int32)


def block_scale(own_key, extent, pieces, smallest, top_value):
    loudness = 1.0
    for axis_at, shards_of in pieces:
        heights = jax.random.uniform(jax.random.fold_in(jax.random.fold_in(own_key, 6), axis_at), (shards_of,), jnp.float32, smallest / len(pieces), top_value / len(pieces))
        loudness = loudness * jnp.repeat(jnp.exp(heights), extent[axis_at] // shards_of).reshape((-1,) + (1,) * (len(extent) - 1 - axis_at))
    return loudness


def centred(rng, extent, deviation, bound, cuts=(), dtype=jnp.bfloat16):
    values = jax.random.normal(rng, extent, jnp.float32) * deviation
    if len(cuts) > 0:
        values = block_scale(rng, extent, cuts, -0.22, 0.18) * values
    return jnp.clip(values, min=-bound, max=bound).astype(dtype)


def setup_inputs(seed: int = 0) -> dict:
    key_of = jax.random.split(jax.random.key(seed), 7)
    return {
        "master": centred(key_of[0], (D, FFW), D ** -0.5, 0.09375, ((0, 128),), jnp.float32),
        "queries": draw_queries(jax.random.fold_in(key_of[6], 71), 0),
        "new_token_key_value": centred(key_of[2], (DECODE_ROWS, DECODE_STEPS, 2, KEY_VALUE_HEADS * HEAD_SIZE), 1.0, 6.0, ((0, 16), (3, 8))),
        "out_weight": centred(key_of[3], (QUERY_HEAD_COUNT * HEAD_SIZE, D), (QUERY_HEAD_COUNT * HEAD_SIZE) ** -0.5, 0.09375, ((0, 8),)),
        "kv_cache": draw_kv_cache(jax.random.fold_in(key_of[6], 71), 0),
        "lengths": draw_lengths(jax.random.fold_in(key_of[6], 71), 0),
    }


def attend(queries, new_token_key_value, kv_cache, lengths):
    rows, steps, width = queries.shape
    head_dim = kv_cache.shape[-1]
    kv_heads = kv_cache.shape[2]
    span = kv_cache.shape[3]
    group = width // head_dim // kv_heads
    fresh = new_token_key_value.reshape(rows, steps, 2, kv_heads, head_dim)
    query_heads = queries.reshape(rows, steps, kv_heads, group, head_dim).astype(jnp.float32)
    scale = 1.0 / math.sqrt(head_dim)
    old_scores = jnp.einsum('rsgqe,rgle->rsgql', query_heads, kv_cache[:, 0].astype(jnp.float32)) * scale
    new_scores = jnp.einsum('rsgqe,rnge->rsgqn', query_heads, fresh[:, :, 0].astype(jnp.float32)) * scale
    old_valid = (jnp.arange(span)[None, :] < lengths[:, None])[:, None, None, None, :]
    new_valid = (jnp.arange(steps)[None, :] <= jnp.arange(steps)[:, None])[None, :, None, None, :]
    old_scores = jnp.where(old_valid, old_scores, jnp.float32(-1e+30))
    new_scores = jnp.where(new_valid, new_scores, jnp.float32(-1e+30))
    top = jnp.maximum(lax.optimization_barrier(jnp.max(old_scores, axis=-1, keepdims=True)), lax.optimization_barrier(jnp.max(new_scores, axis=-1, keepdims=True)))
    old_exp = jnp.exp(old_scores - top)
    new_exp = jnp.exp(new_scores - top)
    total = lax.optimization_barrier(jnp.sum(old_exp, axis=-1, keepdims=True)) + lax.optimization_barrier(jnp.sum(new_exp, axis=-1, keepdims=True))
    old_weights = (old_exp / total).astype(jnp.bfloat16)
    new_weights = (new_exp / total).astype(jnp.bfloat16)
    mixed = jnp.einsum('rsgql,rgle->rsgqe', old_weights.astype(jnp.float32), kv_cache[:, 1].astype(jnp.float32))
    mixed = mixed + jnp.einsum('rsgqn,rnge->rsgqe', new_weights.astype(jnp.float32), fresh[:, :, 1].astype(jnp.float32))
    return mixed.astype(jnp.bfloat16).reshape(rows, steps, width)

def reference(master, queries, new_token_key_value, out_weight, kv_cache, lengths):
    new_weight = master.astype(jnp.bfloat16)
    attn_heads = attend(queries, new_token_key_value, kv_cache, lengths)
    attn_out = jnp.einsum('rsw,wd->rsd', attn_heads.astype(jnp.float32), out_weight.astype(jnp.float32))
    return (new_weight, attn_out.astype(jnp.bfloat16))
```

```python
import math

import jax
import jax.numpy as jnp
from jax import lax
from jax.experimental import pallas as pl
from jax.experimental.pallas import tpu as pltpu
from jax.sharding import PartitionSpec as P

AXES = ("fsdp", "tp")

def send(value, dx=0, dy=0, dz=0, dc=0):
    pairs = []
    for z in range(4):
        for x in range(4):
            for c in range(2):
                for y in range(4):
                    z2, x2, c2, y2 = (z + dz) % 4, (x + dx) % 4, (c + dc) % 2, (y + dy) % 4
                    source = ((z // 2 * 4 + x) * 2 + c) * 8 + z % 2 * 4 + y
                    target = ((z2 // 2 * 4 + x2) * 2 + c2) * 8 + z2 % 2 * 4 + y2
                    pairs.append((source, target))
    return lax.ppermute(value, AXES, pairs)


def cast_blocks(master):
    rows, width = master.shape[0], master.shape[1] // 8

    def kernel(in_ref, out_ref):
        for t in range(8):
            out_ref[t] = in_ref[:, t * width : (t + 1) * width].astype(jnp.bfloat16)

    whole = pl.BlockSpec(memory_space=pltpu.VMEM)
    return pl.pallas_call(
        kernel,
        in_specs=[whole],
        out_specs=whole,
        out_shape=jax.ShapeDtypeStruct((8, rows, width), jnp.bfloat16),
        compiler_params=pltpu.CompilerParams(vmem_limit_bytes=16 << 20),
    )(master)


def attend(queries, fresh, kv_cache, out_weight, lengths, after):
    rows, steps, width = queries.shape
    span, head = kv_cache.shape[3:]
    group = width // head
    part = out_weight.shape[1] // 8
    scale = 1.0 / math.sqrt(head)

    def kernel(lengths_ref, q_ref, fresh_ref, cache_hbm, weight_hbm, after_ref, out_ref, *scratch):
        cache_ref, weight_ref, heads_ref, cache_sem, weight_sem = scratch
        caches = [
            pltpu.make_async_copy(cache_hbm.at[r, :, 0], cache_ref.at[r], cache_sem.at[r])
            for r in range(rows)
        ]
        weights = [
            pltpu.make_async_copy(
                weight_hbm.at[:, pl.ds(t * part, part)], weight_ref.at[t], weight_sem.at[t]
            )
            for t in range(8)
        ]
        for copy in caches + weights:
            copy.start()
        contract = (((1,), (1,)), ((), ()))
        for r in range(rows):
            q = q_ref[r].astype(jnp.float32)
            q = jnp.concatenate([q[:, h * head : (h + 1) * head] for h in range(group)], 0)
            q = q.astype(jnp.bfloat16)
            caches[r].wait()
            old = lax.dot_general(q, cache_ref[r, 0], contract, preferred_element_type=jnp.float32)
            new = lax.dot_general(
                q, fresh_ref[r, :, 0], contract, preferred_element_type=jnp.float32
            )
            place = lax.broadcasted_iota(jnp.int32, old.shape, 1)
            old = jnp.where(place < lengths_ref[r], old * scale, jnp.float32(-1e30))
            step = lax.rem(lax.broadcasted_iota(jnp.int32, new.shape, 0), steps)
            token = lax.broadcasted_iota(jnp.int32, new.shape, 1)
            new = jnp.where(token <= step, new * scale, jnp.float32(-1e30))
            top = jnp.maximum(
                jnp.max(old, axis=1, keepdims=True), jnp.max(new, axis=1, keepdims=True)
            )
            old, new = jnp.exp(old - top), jnp.exp(new - top)
            total = jnp.sum(old, axis=1, keepdims=True) + jnp.sum(new, axis=1, keepdims=True)
            old = (old / total).astype(jnp.bfloat16)
            new = (new / total).astype(jnp.bfloat16)
            mixed = jnp.dot(old, cache_ref[r, 1], preferred_element_type=jnp.float32)
            mixed += jnp.dot(new, fresh_ref[r, :, 1], preferred_element_type=jnp.float32)
            for h in range(group):
                heads_ref[r * steps : (r + 1) * steps, h * head : (h + 1) * head] = mixed[
                    h * steps : (h + 1) * steps
                ]
        heads = heads_ref[...].astype(jnp.bfloat16)
        for t in range(8):
            weights[t].wait()
            out_ref[t % 4, t // 4] = jnp.dot(
                heads, weight_ref[t], preferred_element_type=jnp.float32
            )

    vmem, hbm = pl.BlockSpec(memory_space=pltpu.VMEM), pl.BlockSpec(memory_space=pltpu.HBM)
    return pl.pallas_call(
        kernel,
        in_specs=[
            pl.BlockSpec(memory_space=pltpu.SMEM), vmem, vmem, hbm, hbm,
            pl.BlockSpec(memory_space=pl.ANY),
        ],
        out_specs=vmem,
        out_shape=jax.ShapeDtypeStruct((4, 2, rows * steps, part), jnp.float32),
        scratch_shapes=[
            pltpu.VMEM((rows, 2, span, head), jnp.bfloat16),
            pltpu.VMEM((8, width, part), jnp.bfloat16),
            pltpu.VMEM((rows * steps, width), jnp.float32),
            pltpu.SemaphoreType.DMA((rows,)),
            pltpu.SemaphoreType.DMA((8,)),
        ],
        compiler_params=pltpu.CompilerParams(vmem_limit_bytes=16 << 20),
        cost_estimate=pl.CostEstimate(flops=1, bytes_accessed=1, transcendentals=0),
    )(
        lengths,
        queries,
        fresh,
        pltpu.with_memory_space_constraint(kv_cache, pltpu.HBM),
        pltpu.with_memory_space_constraint(out_weight, pltpu.HBM),
        after,
    )


def place(out, pieces):
    shape = (2, 4, 2, 8) + pieces[0][0].shape[1:]
    index = jnp.stack([jnp.int32(v) for p in pieces for v in p[2:]])
    count = len(pieces)

    def kernel(index_ref, *refs):
        out_ref, sem = refs[-2], refs[-1]
        copies = []
        for k in range(count):
            z, x, c = (index_ref[3 * k + j] for j in range(3))
            target = out_ref.at[z, x, c, pl.ds(pieces[k][1], pieces[k][0].shape[0])]
            copies.append(pltpu.make_async_copy(refs[k], target, sem.at[k]))
        for copy in copies:
            copy.start()
        for copy in copies:
            copy.wait()

    operands = [index] + [p[0] for p in pieces] + ([] if out is None else [out])
    specs = [pl.BlockSpec(memory_space=pltpu.SMEM)]
    specs += [pl.BlockSpec(memory_space=pltpu.VMEM)] * count
    specs += [] if out is None else [pl.BlockSpec(memory_space=pl.ANY)]
    return pl.pallas_call(
        kernel,
        in_specs=specs,
        out_specs=pl.BlockSpec(memory_space=pl.ANY),
        out_shape=jax.ShapeDtypeStruct(shape, jnp.bfloat16),
        scratch_shapes=[pltpu.SemaphoreType.DMA((count,))],
        input_output_aliases={} if out is None else {count + 1: 0},
        compiler_params=pltpu.CompilerParams(vmem_limit_bytes=12 << 20),
    )(*operands)


def fence(*values):
    def kernel(*refs):
        pass

    made = pl.pallas_call(
        kernel,
        in_specs=[pl.BlockSpec(memory_space=pl.ANY)] * len(values),
        out_specs=[pl.BlockSpec(memory_space=pl.ANY)] * len(values),
        out_shape=[jax.ShapeDtypeStruct(v.shape, v.dtype) for v in values],
        input_output_aliases={k: k for k in range(len(values))},
        compiler_params=pltpu.CompilerParams(vmem_limit_bytes=1 << 20),
    )(*values)
    return made if len(values) > 1 else made[0]


def local(master, queries, new_token_key_value, out_weight, kv_cache, lengths):
    f, t = lax.axis_index("fsdp"), lax.axis_index("tp")
    z_hi, x, core = f // 8, f // 2 % 4, f % 2
    z_lo = t // 4
    width = master.shape[1] // 8
    blocks = cast_blocks(master)

    def swap(piece):
        with jax.named_scope("core"):
            return send(piece, dc=1)

    def both(piece, z, hop, first=0):
        place_x = (x - hop) % 4
        return [(piece, first, z, place_x, core), (swap(piece), first, z, place_x, 1 - core)]

    def pick(value, index):
        return lax.dynamic_index_in_dim(value, index, 0, keepdims=False)

    with jax.named_scope("over_t"):
        own = lax.all_to_all(blocks, "tp", split_axis=0, concat_axis=0, tiled=True)
    r, s, w = queries.shape
    shares = attend(queries, new_token_key_value, kv_cache, out_weight, lengths, blocks)
    own, shares = fence(own, shares)

    with jax.named_scope("own_x"):
        own_1, own_3 = send(own, dx=1), send(own, dx=-1)
    with jax.named_scope("over_z"):
        dup = send(own, dz=2)
    with jax.named_scope("sum_y"):
        shares = lax.all_to_all(
            shares, "tp", split_axis=0, concat_axis=0, tiled=True,
            axis_index_groups=((0, 1, 2, 3), (4, 5, 6, 7)),
        )
    out = place(None, both(own, z_hi, 0))
    own_1, own_3, shares, out = fence(own_1, own_3, shares, out)

    with jax.named_scope("own_x2"):
        own_2, own_2b = send(own_1[:4], dx=1), send(own_3[4:], dx=-1)
    with jax.named_scope("dup_x"):
        dup_1, dup_3 = send(dup, dx=1), send(dup, dx=-1)
    with jax.named_scope("sum_z"):
        total = jnp.sum(shares, axis=0)
        pairs = [(i, i // 8 * 8 + (i + 4) % 8) for i in range(128)]
        attn = pick(total, z_lo) + lax.ppermute(pick(total, 1 - z_lo), AXES, pairs)
        attn = attn.astype(jnp.bfloat16)
    out = place(out, both(own_1, z_hi, 1) + both(own_3, z_hi, 3))
    own_2, own_2b, attn, out = fence(own_2, own_2b, attn, out)

    with jax.named_scope("over_z2"):
        dup_2, dup_2b = send(own_2, dz=2), send(own_2b, dz=2)
    out = place(out, both(dup, 1 - z_hi, 0) + both(own_2, z_hi, 2) + both(own_2b, z_hi, 2, 4))
    dup_1, dup_2, dup_2b, dup_3, out = fence(dup_1, dup_2, dup_2b, dup_3, out)

    pairs = [both(dup_1, 1 - z_hi, 1), both(dup_3, 1 - z_hi, 3)]
    pairs += [both(dup_2, 1 - z_hi, 2), both(dup_2b, 1 - z_hi, 2, 4)]
    out = place(out, [mine for mine, _ in pairs])
    out = place(out, [theirs for _, theirs in pairs])
    return (out.reshape(-1, width), attn.reshape(r, s, -1))


def solution(mesh):
    in_specs = (
        P(("fsdp", "tp"), None),
        P("fsdp", None, "tp"),
        P("fsdp", None, None, "tp"),
        P("tp", None),
        P("fsdp", None, "tp", None, None),
        P("fsdp"),
    )
    out_specs = (P(None, "tp"), P("fsdp", None, "tp"))
    return jax.shard_map(local, mesh=mesh, in_specs=in_specs, out_specs=out_specs, check_vma=False)
```

```python
import math

import jax
import jax.numpy as jnp
from jax import lax
from jax.experimental import pallas as pl
from jax.experimental.pallas import tpu as pltpu
from jax.sharding import PartitionSpec as P

AXES = ("fsdp", "tp")

def send(value, dx=0, dy=0, dz=0, dc=0):
    pairs = []
    for z in range(4):
        for x in range(4):
            for c in range(2):
                for y in range(4):
                    z2, x2, c2, y2 = (z + dz) % 4, (x + dx) % 4, (c + dc) % 2, (y + dy) % 4
                    source = ((z // 2 * 4 + x) * 2 + c) * 8 + z % 2 * 4 + y
                    target = ((z2 // 2 * 4 + x2) * 2 + c2) * 8 + z2 % 2 * 4 + y2
                    pairs.append((source, target))
    return lax.ppermute(value, AXES, pairs)


def cast_blocks(master):
    rows, width = master.shape[0], master.shape[1] // 8

    def kernel(in_ref, out_ref):
        for t in range(8):
            out_ref[t] = in_ref[:, t * width : (t + 1) * width].astype(jnp.bfloat16)

    whole = pl.BlockSpec(memory_space=pltpu.VMEM)
    return pl.pallas_call(
        kernel,
        in_specs=[whole],
        out_specs=whole,
        out_shape=jax.ShapeDtypeStruct((8, rows, width), jnp.bfloat16),
        compiler_params=pltpu.CompilerParams(vmem_limit_bytes=16 << 20),
    )(master)


def attend(queries, fresh, kv_cache, out_weight, lengths, after):
    rows, steps, width = queries.shape
    span, head = kv_cache.shape[3:]
    group = width // head
    part = out_weight.shape[1] // 8
    scale = 1.0 / math.sqrt(head)

    def kernel(lengths_ref, q_ref, fresh_ref, cache_hbm, weight_hbm, after_ref, out_ref, *scratch):
        cache_ref, weight_ref, heads_ref, cache_sem, weight_sem = scratch
        caches = [
            pltpu.make_async_copy(cache_hbm.at[r, :, 0], cache_ref.at[r], cache_sem.at[r])
            for r in range(rows)
        ]
        weights = [
            pltpu.make_async_copy(
                weight_hbm.at[:, pl.ds(t * part, part)], weight_ref.at[t], weight_sem.at[t]
            )
            for t in range(8)
        ]
        for copy in caches + weights:
            copy.start()
        contract = (((1,), (1,)), ((), ()))
        for r in range(rows):
            q = q_ref[r].astype(jnp.float32)
            q = jnp.concatenate([q[:, h * head : (h + 1) * head] for h in range(group)], 0)
            q = q.astype(jnp.bfloat16)
            caches[r].wait()
            old = lax.dot_general(q, cache_ref[r, 0], contract, preferred_element_type=jnp.float32)
            new = lax.dot_general(
                q, fresh_ref[r, :, 0], contract, preferred_element_type=jnp.float32
            )
            place = lax.broadcasted_iota(jnp.int32, old.shape, 1)
            old = jnp.where(place < lengths_ref[r], old * scale, jnp.float32(-1e30))
            step = lax.rem(lax.broadcasted_iota(jnp.int32, new.shape, 0), steps)
            token = lax.broadcasted_iota(jnp.int32, new.shape, 1)
            new = jnp.where(token <= step, new * scale, jnp.float32(-1e30))
            top = jnp.maximum(
                jnp.max(old, axis=1, keepdims=True), jnp.max(new, axis=1, keepdims=True)
            )
            old, new = jnp.exp(old - top), jnp.exp(new - top)
            total = jnp.sum(old, axis=1, keepdims=True) + jnp.sum(new, axis=1, keepdims=True)
            old = (old / total).astype(jnp.bfloat16)
            new = (new / total).astype(jnp.bfloat16)
            mixed = jnp.dot(old, cache_ref[r, 1], preferred_element_type=jnp.float32)
            mixed += jnp.dot(new, fresh_ref[r, :, 1], preferred_element_type=jnp.float32)
            for h in range(group):
                heads_ref[r * steps : (r + 1) * steps, h * head : (h + 1) * head] = mixed[
                    h * steps : (h + 1) * steps
                ]
        heads = heads_ref[...].astype(jnp.bfloat16)
        for t in range(8):
            weights[t].wait()
            out_ref[t % 4, t // 4] = jnp.dot(
                heads, weight_ref[t], preferred_element_type=jnp.float32
            )

    vmem, hbm = pl.BlockSpec(memory_space=pltpu.VMEM), pl.BlockSpec(memory_space=pltpu.HBM)
    return pl.pallas_call(
        kernel,
        in_specs=[
            pl.BlockSpec(memory_space=pltpu.SMEM), vmem, vmem, hbm, hbm,
            pl.BlockSpec(memory_space=pl.ANY),
        ],
        out_specs=vmem,
        out_shape=jax.ShapeDtypeStruct((4, 2, rows * steps, part), jnp.float32),
        scratch_shapes=[
            pltpu.VMEM((rows, 2, span, head), jnp.bfloat16),
            pltpu.VMEM((8, width, part), jnp.bfloat16),
            pltpu.VMEM((rows * steps, width), jnp.float32),
            pltpu.SemaphoreType.DMA((rows,)),
            pltpu.SemaphoreType.DMA((8,)),
        ],
        compiler_params=pltpu.CompilerParams(vmem_limit_bytes=16 << 20),
        cost_estimate=pl.CostEstimate(flops=1, bytes_accessed=1, transcendentals=0),
    )(
        lengths,
        queries,
        fresh,
        pltpu.with_memory_space_constraint(kv_cache, pltpu.HBM),
        pltpu.with_memory_space_constraint(out_weight, pltpu.HBM),
        after,
    )


def place(out, pieces):
    shape = (2, 4, 2, 8) + pieces[0][0].shape[1:]
    index = jnp.stack([jnp.int32(v) for p in pieces for v in p[2:]])
    count = len(pieces)

    def kernel(index_ref, *refs):
        out_ref, sem = refs[-2], refs[-1]
        copies = []
        for k in range(count):
            z, x, c = (index_ref[3 * k + j] for j in range(3))
            target = out_ref.at[z, x, c, pl.ds(pieces[k][1], pieces[k][0].shape[0])]
            copies.append(pltpu.make_async_copy(refs[k], target, sem.at[k]))
        for copy in copies:
            copy.start()
        for copy in copies:
            copy.wait()

    operands = [index] + [p[0] for p in pieces] + ([] if out is None else [out])
    specs = [pl.BlockSpec(memory_space=pltpu.SMEM)]
    specs += [pl.BlockSpec(memory_space=pltpu.VMEM)] * count
    specs += [] if out is None else [pl.BlockSpec(memory_space=pl.ANY)]
    return pl.pallas_call(
        kernel,
        in_specs=specs,
        out_specs=pl.BlockSpec(memory_space=pl.ANY),
        out_shape=jax.ShapeDtypeStruct(shape, jnp.bfloat16),
        scratch_shapes=[pltpu.SemaphoreType.DMA((count,))],
        input_output_aliases={} if out is None else {count + 1: 0},
        compiler_params=pltpu.CompilerParams(vmem_limit_bytes=12 << 20),
    )(*operands)


def fence(*values, cost=0):
    def kernel(*refs):
        pass

    made = pl.pallas_call(
        kernel,
        in_specs=[pl.BlockSpec(memory_space=pl.ANY)] * len(values),
        out_specs=[pl.BlockSpec(memory_space=pl.ANY)] * len(values),
        out_shape=[jax.ShapeDtypeStruct(v.shape, v.dtype) for v in values],
        input_output_aliases={k: k for k in range(len(values))},
        compiler_params=pltpu.CompilerParams(vmem_limit_bytes=1 << 20),
        cost_estimate=pl.CostEstimate(flops=0, bytes_accessed=cost, transcendentals=0),
    )(*values)
    return made if len(values) > 1 else made[0]


def local(master, queries, new_token_key_value, out_weight, kv_cache, lengths):
    f, t = lax.axis_index("fsdp"), lax.axis_index("tp")
    z_hi, x, core = f // 8, f // 2 % 4, f % 2
    z_lo = t // 4
    width = master.shape[1] // 8
    blocks = cast_blocks(master)

    def swap(piece):
        with jax.named_scope("core"):
            return send(piece, dc=1)

    def both(piece, z, hop, first=0):
        place_x = (x - hop) % 4
        return [(piece, first, z, place_x, core), (swap(piece), first, z, place_x, 1 - core)]

    def pick(value, index):
        return lax.dynamic_index_in_dim(value, index, 0, keepdims=False)

    with jax.named_scope("over_t"):
        own = lax.all_to_all(blocks, "tp", split_axis=0, concat_axis=0, tiled=True)
    r, s, w = queries.shape
    shares = attend(queries, new_token_key_value, kv_cache, out_weight, lengths, blocks)
    own, shares = fence(own, shares)

    with jax.named_scope("own_x"):
        own_1, own_3 = send(own, dx=1), send(own, dx=-1)
    with jax.named_scope("over_z"):
        dup = send(own, dz=2)
    with jax.named_scope("sum_y"):
        shares = lax.all_to_all(
            shares, "tp", split_axis=0, concat_axis=0, tiled=True,
            axis_index_groups=((0, 1, 2, 3), (4, 5, 6, 7)),
        )
    out = place(None, both(own, z_hi, 0))
    own_1, own_3, shares, out = fence(own_1, own_3, shares, out)

    low_1, high_3 = own_1[:4], own_3[4:]
    with jax.named_scope("own_x2"):
        low_2, high_2 = send(low_1, dx=1), send(high_3, dx=-1)
    with jax.named_scope("dup_z"):
        dup_low_1 = send(low_1, dz=2)
    with jax.named_scope("dup_x"):
        dup_high_1, dup_3 = send(dup[4:], dx=1), send(dup, dx=-1)
        dup_high_1 = fence(dup_high_1, cost=1 << 20)
    out = place(out, both(own_1, z_hi, 1) + both(own_3, z_hi, 3))
    low_2, high_2, dup_low_1, shares, out = fence(low_2, high_2, dup_low_1, shares, out)

    with jax.named_scope("dup_x2"):
        dup_low_2 = send(dup_low_1, dx=1)
    with jax.named_scope("dup_z2"):
        dup_high_2 = send(high_2, dz=2)
    total = jnp.sum(shares, axis=0)
    kept, given = pick(total, z_lo), pick(total, 1 - z_lo)
    out = place(out, both(dup, 1 - z_hi, 0) + both(low_2, z_hi, 2) + both(high_2, z_hi, 2, 4))
    out = place(out, both(dup_low_1, 1 - z_hi, 1))
    dup_high_1, dup_3, dup_low_2, dup_high_2, kept, given, out = fence(
        dup_high_1, dup_3, dup_low_2, dup_high_2, kept, given, out
    )

    pairs = [both(dup_high_1, 1 - z_hi, 1, 4), both(dup_3, 1 - z_hi, 3)]
    pairs += [both(dup_low_2, 1 - z_hi, 2), both(dup_high_2, 1 - z_hi, 2, 4)]
    out = place(out, [mine for mine, _ in pairs])
    out = place(out, [theirs for _, theirs in pairs])
    with jax.named_scope("sum_z"):
        attn = kept + lax.ppermute(given, AXES, [(i, i ^ 4) for i in range(128)])
        attn = attn.astype(jnp.bfloat16)
    return (out.reshape(-1, width), attn.reshape(r, s, -1))


def solution(mesh):
    in_specs = (
        P(("fsdp", "tp"), None),
        P("fsdp", None, "tp"),
        P("fsdp", None, None, "tp"),
        P("tp", None),
        P("fsdp", None, "tp", None, None),
        P("fsdp"),
    )
    out_specs = (P(None, "tp"), P("fsdp", None, "tp"))
    return jax.shard_map(local, mesh=mesh, in_specs=in_specs, out_specs=out_specs, check_vma=False)
```

```python
import math

import jax
import jax.numpy as jnp
from jax import lax
from jax.experimental import pallas as pl
from jax.experimental.pallas import tpu as pltpu
from jax.sharding import PartitionSpec as P

AXES = ("fsdp", "tp")

def send(value, dx=0, dy=0, dz=0, dc=0):
    pairs = []
    for z in range(4):
        for x in range(4):
            for c in range(2):
                for y in range(4):
                    z2, x2, c2, y2 = (z + dz) % 4, (x + dx) % 4, (c + dc) % 2, (y + dy) % 4
                    source = ((z // 2 * 4 + x) * 2 + c) * 8 + z % 2 * 4 + y
                    target = ((z2 // 2 * 4 + x2) * 2 + c2) * 8 + z2 % 2 * 4 + y2
                    pairs.append((source, target))
    return lax.ppermute(value, AXES, pairs)


def cast_blocks(master):
    rows, width = master.shape[0], master.shape[1] // 8

    def kernel(in_ref, out_ref):
        for t in range(8):
            out_ref[t] = in_ref[:, t * width : (t + 1) * width].astype(jnp.bfloat16)

    whole = pl.BlockSpec(memory_space=pltpu.VMEM)
    return pl.pallas_call(
        kernel,
        in_specs=[whole],
        out_specs=whole,
        out_shape=jax.ShapeDtypeStruct((8, rows, width), jnp.bfloat16),
        compiler_params=pltpu.CompilerParams(vmem_limit_bytes=16 << 20),
    )(master)


def attend(queries, fresh, kv_cache, out_weight, lengths, after):
    rows, steps, width = queries.shape
    span, head = kv_cache.shape[3:]
    group = width // head
    part = out_weight.shape[1] // 8
    scale = 1.0 / math.sqrt(head)

    def kernel(lengths_ref, q_ref, fresh_ref, cache_hbm, weight_hbm, after_ref, out_ref, *scratch):
        cache_ref, weight_ref, heads_ref, cache_sem, weight_sem = scratch
        caches = [
            pltpu.make_async_copy(cache_hbm.at[r, :, 0], cache_ref.at[r], cache_sem.at[r])
            for r in range(rows)
        ]
        weights = [
            pltpu.make_async_copy(
                weight_hbm.at[:, pl.ds(t * part, part)], weight_ref.at[t], weight_sem.at[t]
            )
            for t in range(8)
        ]
        for copy in caches + weights:
            copy.start()
        contract = (((1,), (1,)), ((), ()))
        for r in range(rows):
            q = q_ref[r].astype(jnp.float32)
            q = jnp.concatenate([q[:, h * head : (h + 1) * head] for h in range(group)], 0)
            q = q.astype(jnp.bfloat16)
            caches[r].wait()
            old = lax.dot_general(q, cache_ref[r, 0], contract, preferred_element_type=jnp.float32)
            new = lax.dot_general(
                q, fresh_ref[r, :, 0], contract, preferred_element_type=jnp.float32
            )
            place = lax.broadcasted_iota(jnp.int32, old.shape, 1)
            old = jnp.where(place < lengths_ref[r], old * scale, jnp.float32(-1e30))
            step = lax.rem(lax.broadcasted_iota(jnp.int32, new.shape, 0), steps)
            token = lax.broadcasted_iota(jnp.int32, new.shape, 1)
            new = jnp.where(token <= step, new * scale, jnp.float32(-1e30))
            top = jnp.maximum(
                jnp.max(old, axis=1, keepdims=True), jnp.max(new, axis=1, keepdims=True)
            )
            old, new = jnp.exp(old - top), jnp.exp(new - top)
            total = jnp.sum(old, axis=1, keepdims=True) + jnp.sum(new, axis=1, keepdims=True)
            old = (old / total).astype(jnp.bfloat16)
            new = (new / total).astype(jnp.bfloat16)
            mixed = jnp.dot(old, cache_ref[r, 1], preferred_element_type=jnp.float32)
            mixed += jnp.dot(new, fresh_ref[r, :, 1], preferred_element_type=jnp.float32)
            for h in range(group):
                heads_ref[r * steps : (r + 1) * steps, h * head : (h + 1) * head] = mixed[
                    h * steps : (h + 1) * steps
                ]
        heads = heads_ref[...].astype(jnp.bfloat16)
        for t in range(8):
            weights[t].wait()
            out_ref[t % 4, t // 4] = jnp.dot(
                heads, weight_ref[t], preferred_element_type=jnp.float32
            )

    vmem, hbm = pl.BlockSpec(memory_space=pltpu.VMEM), pl.BlockSpec(memory_space=pltpu.HBM)
    return pl.pallas_call(
        kernel,
        in_specs=[
            pl.BlockSpec(memory_space=pltpu.SMEM), vmem, vmem, hbm, hbm,
            pl.BlockSpec(memory_space=pl.ANY),
        ],
        out_specs=vmem,
        out_shape=jax.ShapeDtypeStruct((4, 2, rows * steps, part), jnp.float32),
        scratch_shapes=[
            pltpu.VMEM((rows, 2, span, head), jnp.bfloat16),
            pltpu.VMEM((8, width, part), jnp.bfloat16),
            pltpu.VMEM((rows * steps, width), jnp.float32),
            pltpu.SemaphoreType.DMA((rows,)),
            pltpu.SemaphoreType.DMA((8,)),
        ],
        compiler_params=pltpu.CompilerParams(vmem_limit_bytes=16 << 20),
        cost_estimate=pl.CostEstimate(flops=1, bytes_accessed=1, transcendentals=0),
    )(
        lengths,
        queries,
        fresh,
        pltpu.with_memory_space_constraint(kv_cache, pltpu.HBM),
        pltpu.with_memory_space_constraint(out_weight, pltpu.HBM),
        after,
    )


def halves(left, right):
    shape = (left.shape[0] // 2,) + left.shape[1:]

    def kernel(left_ref, right_ref, low_ref, high_ref, sem):
        half = shape[0]
        copies = [
            pltpu.make_async_copy(left_ref.at[pl.ds(0, half)], low_ref, sem.at[0]),
            pltpu.make_async_copy(right_ref.at[pl.ds(half, half)], high_ref, sem.at[1]),
        ]
        for copy in copies:
            copy.start()
        for copy in copies:
            copy.wait()

    return pl.pallas_call(
        kernel,
        in_specs=[pl.BlockSpec(memory_space=pl.ANY)] * 2,
        out_specs=[pl.BlockSpec(memory_space=pltpu.VMEM)] * 2,
        out_shape=[jax.ShapeDtypeStruct(shape, left.dtype)] * 2,
        scratch_shapes=[pltpu.SemaphoreType.DMA((2,))],
        compiler_params=pltpu.CompilerParams(vmem_limit_bytes=4 << 20),
        cost_estimate=pl.CostEstimate(flops=0, bytes_accessed=0, transcendentals=0),
    )(left, right)


def place(out, pieces):
    shape = (2, 4, 2, 8) + pieces[0][0].shape[1:]
    index = jnp.stack([jnp.int32(v) for p in pieces for v in p[2:]])
    count = len(pieces)

    def kernel(index_ref, *refs):
        out_ref, sem = refs[-2], refs[-1]
        copies = []
        for k in range(count):
            z, x, c = (index_ref[3 * k + j] for j in range(3))
            target = out_ref.at[z, x, c, pl.ds(pieces[k][1], pieces[k][0].shape[0])]
            copies.append(pltpu.make_async_copy(refs[k], target, sem.at[k]))
        for copy in copies:
            copy.start()
        for copy in copies:
            copy.wait()

    operands = [index] + [p[0] for p in pieces] + ([] if out is None else [out])
    specs = [pl.BlockSpec(memory_space=pltpu.SMEM)]
    specs += [pl.BlockSpec(memory_space=pltpu.VMEM)] * count
    specs += [] if out is None else [pl.BlockSpec(memory_space=pl.ANY)]
    return pl.pallas_call(
        kernel,
        in_specs=specs,
        out_specs=pl.BlockSpec(memory_space=pl.ANY),
        out_shape=jax.ShapeDtypeStruct(shape, jnp.bfloat16),
        scratch_shapes=[pltpu.SemaphoreType.DMA((count,))],
        input_output_aliases={} if out is None else {count + 1: 0},
        compiler_params=pltpu.CompilerParams(vmem_limit_bytes=12 << 20),
    )(*operands)


def fence(*values, cost=0):
    def kernel(*refs):
        pass

    made = pl.pallas_call(
        kernel,
        in_specs=[pl.BlockSpec(memory_space=pl.ANY)] * len(values),
        out_specs=[pl.BlockSpec(memory_space=pl.ANY)] * len(values),
        out_shape=[jax.ShapeDtypeStruct(v.shape, v.dtype) for v in values],
        input_output_aliases={k: k for k in range(len(values))},
        compiler_params=pltpu.CompilerParams(vmem_limit_bytes=1 << 20),
        cost_estimate=pl.CostEstimate(flops=0, bytes_accessed=cost, transcendentals=0),
    )(*values)
    return made if len(values) > 1 else made[0]


def local(master, queries, new_token_key_value, out_weight, kv_cache, lengths):
    f, t = lax.axis_index("fsdp"), lax.axis_index("tp")
    z_hi, x, core = f // 8, f // 2 % 4, f % 2
    z_lo = t // 4
    width = master.shape[1] // 8
    blocks = cast_blocks(master)

    def swap(piece):
        with jax.named_scope("core"):
            return send(piece, dc=1)

    def both(piece, z, hop, first=0):
        place_x = (x - hop) % 4
        return [(piece, first, z, place_x, core), (swap(piece), first, z, place_x, 1 - core)]

    def pick(value, index):
        return lax.dynamic_index_in_dim(value, index, 0, keepdims=False)

    with jax.named_scope("over_t"):
        own = lax.all_to_all(blocks, "tp", split_axis=0, concat_axis=0, tiled=True)
    r, s, w = queries.shape
    shares = attend(queries, new_token_key_value, kv_cache, out_weight, lengths, blocks)
    own, shares = fence(own, shares)

    with jax.named_scope("own_x"):
        own_1, own_3 = send(own, dx=1), send(own, dx=-1)
    with jax.named_scope("over_z"):
        dup = send(own, dz=2)
    with jax.named_scope("sum_y"):
        shares = lax.all_to_all(
            shares, "tp", split_axis=0, concat_axis=0, tiled=True,
            axis_index_groups=((0, 1, 2, 3), (4, 5, 6, 7)),
        )
    out = place(None, both(own, z_hi, 0))
    own_1, own_3, shares, out = fence(own_1, own_3, shares, out)

    low_1, high_3 = halves(own_1, own_3)
    with jax.named_scope("own_x2"):
        low_2, high_2 = send(low_1, dx=1), send(high_3, dx=-1)
    with jax.named_scope("dup_z"):
        dup_low_1 = send(low_1, dz=2)
    with jax.named_scope("dup_x"):
        dup_high_1, dup_3 = send(dup[4:], dx=1), send(dup, dx=-1)
        dup_high_1 = fence(dup_high_1, cost=1 << 20)
    out = place(out, both(own_1, z_hi, 1) + both(own_3, z_hi, 3))
    low_2, high_2, dup_low_1, shares, out = fence(low_2, high_2, dup_low_1, shares, out)

    with jax.named_scope("dup_x2"):
        dup_low_2 = send(dup_low_1, dx=1)
    with jax.named_scope("dup_z2"):
        dup_high_2 = send(high_2, dz=2)
    total = jnp.sum(shares, axis=0)
    kept, given = pick(total, z_lo), pick(total, 1 - z_lo)
    out = place(out, both(dup_low_1, 1 - z_hi, 1))
    out = place(out, both(dup, 1 - z_hi, 0) + both(low_2, z_hi, 2) + both(high_2, z_hi, 2, 4))
    dup_high_1, dup_3, dup_low_2, dup_high_2, kept, given, out = fence(
        dup_high_1, dup_3, dup_low_2, dup_high_2, kept, given, out
    )

    with jax.named_scope("sum_z"):
        given = lax.ppermute(given, AXES, [(i, i ^ 4) for i in range(128)])
    pairs = [both(dup_high_1, 1 - z_hi, 1, 4), both(dup_3, 1 - z_hi, 3)]
    pairs += [both(dup_low_2, 1 - z_hi, 2), both(dup_high_2, 1 - z_hi, 2, 4)]
    out = place(out, [mine for mine, _ in pairs])
    out = place(out, [theirs for _, theirs in pairs])
    out, kept, given = fence(out, kept, given)
    attn = (kept + given).astype(jnp.bfloat16)
    return (out.reshape(-1, width), attn.reshape(r, s, -1))


def solution(mesh):
    in_specs = (
        P(("fsdp", "tp"), None),
        P("fsdp", None, "tp"),
        P("fsdp", None, None, "tp"),
        P("tp", None),
        P("fsdp", None, "tp", None, None),
        P("fsdp"),
    )
    out_specs = (P(None, "tp"), P("fsdp", None, "tp"))
    return jax.shard_map(local, mesh=mesh, in_specs=in_specs, out_specs=out_specs, check_vma=False)
```

```python
import math

import jax
import jax.numpy as jnp
from jax import lax
from jax.experimental import pallas as pl
from jax.experimental.pallas import tpu as pltpu
from jax.sharding import PartitionSpec as P

AXES = ("fsdp", "tp")

def send(value, dx=0, dy=0, dz=0, dc=0):
    pairs = []
    for z in range(4):
        for x in range(4):
            for c in range(2):
                for y in range(4):
                    z2, x2, c2, y2 = (z + dz) % 4, (x + dx) % 4, (c + dc) % 2, (y + dy) % 4
                    source = ((z // 2 * 4 + x) * 2 + c) * 8 + z % 2 * 4 + y
                    target = ((z2 // 2 * 4 + x2) * 2 + c2) * 8 + z2 % 2 * 4 + y2
                    pairs.append((source, target))
    return lax.ppermute(value, AXES, pairs)


def cast_blocks(master):
    rows, width = master.shape[0], master.shape[1] // 8

    def kernel(in_ref, out_ref):
        for t in range(8):
            out_ref[t] = in_ref[:, t * width : (t + 1) * width].astype(jnp.bfloat16)

    whole = pl.BlockSpec(memory_space=pltpu.VMEM)
    return pl.pallas_call(
        kernel,
        in_specs=[whole],
        out_specs=whole,
        out_shape=jax.ShapeDtypeStruct((8, rows, width), jnp.bfloat16),
        compiler_params=pltpu.CompilerParams(vmem_limit_bytes=16 << 20),
    )(master)


def attend(queries, fresh, kv_cache, out_weight, lengths, after):
    rows, steps, width = queries.shape
    span, head = kv_cache.shape[3:]
    group = width // head
    part = out_weight.shape[1] // 8
    scale = 1.0 / math.sqrt(head)

    def kernel(lengths_ref, q_ref, fresh_ref, cache_hbm, weight_hbm, after_ref, out_ref, *scratch):
        cache_ref, weight_ref, heads_ref, cache_sem, weight_sem = scratch
        caches = [
            pltpu.make_async_copy(cache_hbm.at[r, :, 0], cache_ref.at[r], cache_sem.at[r])
            for r in range(rows)
        ]
        weights = [
            pltpu.make_async_copy(
                weight_hbm.at[:, pl.ds(t * part, part)], weight_ref.at[t], weight_sem.at[t]
            )
            for t in range(8)
        ]
        for copy in caches + weights:
            copy.start()
        contract = (((1,), (1,)), ((), ()))
        for r in range(rows):
            q = q_ref[r].astype(jnp.float32)
            q = jnp.concatenate([q[:, h * head : (h + 1) * head] for h in range(group)], 0)
            q = q.astype(jnp.bfloat16)
            caches[r].wait()
            old = lax.dot_general(q, cache_ref[r, 0], contract, preferred_element_type=jnp.float32)
            new = lax.dot_general(
                q, fresh_ref[r, :, 0], contract, preferred_element_type=jnp.float32
            )
            place = lax.broadcasted_iota(jnp.int32, old.shape, 1)
            old = jnp.where(place < lengths_ref[r], old * scale, jnp.float32(-1e30))
            step = lax.rem(lax.broadcasted_iota(jnp.int32, new.shape, 0), steps)
            token = lax.broadcasted_iota(jnp.int32, new.shape, 1)
            new = jnp.where(token <= step, new * scale, jnp.float32(-1e30))
            top = jnp.maximum(
                jnp.max(old, axis=1, keepdims=True), jnp.max(new, axis=1, keepdims=True)
            )
            old, new = jnp.exp(old - top), jnp.exp(new - top)
            total = jnp.sum(old, axis=1, keepdims=True) + jnp.sum(new, axis=1, keepdims=True)
            old = (old / total).astype(jnp.bfloat16)
            new = (new / total).astype(jnp.bfloat16)
            mixed = jnp.dot(old, cache_ref[r, 1], preferred_element_type=jnp.float32)
            mixed += jnp.dot(new, fresh_ref[r, :, 1], preferred_element_type=jnp.float32)
            for h in range(group):
                heads_ref[r * steps : (r + 1) * steps, h * head : (h + 1) * head] = mixed[
                    h * steps : (h + 1) * steps
                ]
        heads = heads_ref[...].astype(jnp.bfloat16)
        for t in range(8):
            weights[t].wait()
            out_ref[t % 4, t // 4] = jnp.dot(
                heads, weight_ref[t], preferred_element_type=jnp.float32
            )

    vmem, hbm = pl.BlockSpec(memory_space=pltpu.VMEM), pl.BlockSpec(memory_space=pltpu.HBM)
    return pl.pallas_call(
        kernel,
        in_specs=[
            pl.BlockSpec(memory_space=pltpu.SMEM), vmem, vmem, hbm, hbm,
            pl.BlockSpec(memory_space=pl.ANY),
        ],
        out_specs=vmem,
        out_shape=jax.ShapeDtypeStruct((4, 2, rows * steps, part), jnp.float32),
        scratch_shapes=[
            pltpu.VMEM((rows, 2, span, head), jnp.bfloat16),
            pltpu.VMEM((8, width, part), jnp.bfloat16),
            pltpu.VMEM((rows * steps, width), jnp.float32),
            pltpu.SemaphoreType.DMA((rows,)),
            pltpu.SemaphoreType.DMA((8,)),
        ],
        compiler_params=pltpu.CompilerParams(vmem_limit_bytes=16 << 20),
        cost_estimate=pl.CostEstimate(flops=1, bytes_accessed=1, transcendentals=0),
    )(
        lengths,
        queries,
        fresh,
        pltpu.with_memory_space_constraint(kv_cache, pltpu.HBM),
        pltpu.with_memory_space_constraint(out_weight, pltpu.HBM),
        after,
    )


def halves(left, right):
    shape = (left.shape[0] // 2,) + left.shape[1:]

    def kernel(left_ref, right_ref, low_ref, high_ref, sem):
        half = shape[0]
        copies = [
            pltpu.make_async_copy(left_ref.at[pl.ds(0, half)], low_ref, sem.at[0]),
            pltpu.make_async_copy(right_ref.at[pl.ds(half, half)], high_ref, sem.at[1]),
        ]
        for copy in copies:
            copy.start()
        for copy in copies:
            copy.wait()

    return pl.pallas_call(
        kernel,
        in_specs=[pl.BlockSpec(memory_space=pl.ANY)] * 2,
        out_specs=[pl.BlockSpec(memory_space=pltpu.VMEM)] * 2,
        out_shape=[jax.ShapeDtypeStruct(shape, left.dtype)] * 2,
        scratch_shapes=[pltpu.SemaphoreType.DMA((2,))],
        compiler_params=pltpu.CompilerParams(vmem_limit_bytes=4 << 20),
        cost_estimate=pl.CostEstimate(flops=0, bytes_accessed=0, transcendentals=0),
    )(left, right)


def place(out, pieces):
    shape = (2, 4, 2, 8) + pieces[0][0].shape[1:]
    index = jnp.stack([jnp.int32(v) for p in pieces for v in p[2:]])
    count = len(pieces)

    def kernel(index_ref, *refs):
        out_ref, sem = refs[-2], refs[-1]
        copies = []
        for k in range(count):
            z, x, c = (index_ref[3 * k + j] for j in range(3))
            target = out_ref.at[z, x, c, pl.ds(pieces[k][1], pieces[k][0].shape[0])]
            copies.append(pltpu.make_async_copy(refs[k], target, sem.at[k]))
        for copy in copies:
            copy.start()
        for copy in copies:
            copy.wait()

    operands = [index] + [p[0] for p in pieces] + ([] if out is None else [out])
    specs = [pl.BlockSpec(memory_space=pltpu.SMEM)]
    specs += [pl.BlockSpec(memory_space=pltpu.VMEM)] * count
    specs += [] if out is None else [pl.BlockSpec(memory_space=pl.ANY)]
    return pl.pallas_call(
        kernel,
        in_specs=specs,
        out_specs=pl.BlockSpec(memory_space=pl.ANY),
        out_shape=jax.ShapeDtypeStruct(shape, jnp.bfloat16),
        scratch_shapes=[pltpu.SemaphoreType.DMA((count,))],
        input_output_aliases={} if out is None else {count + 1: 0},
        compiler_params=pltpu.CompilerParams(vmem_limit_bytes=12 << 20),
    )(*operands)


def fence(*values, cost=0):
    def kernel(*refs):
        pass

    made = pl.pallas_call(
        kernel,
        in_specs=[pl.BlockSpec(memory_space=pl.ANY)] * len(values),
        out_specs=[pl.BlockSpec(memory_space=pl.ANY)] * len(values),
        out_shape=[jax.ShapeDtypeStruct(v.shape, v.dtype) for v in values],
        input_output_aliases={k: k for k in range(len(values))},
        compiler_params=pltpu.CompilerParams(vmem_limit_bytes=1 << 20),
        cost_estimate=pl.CostEstimate(flops=0, bytes_accessed=cost, transcendentals=0),
    )(*values)
    return made if len(values) > 1 else made[0]


def local(master, queries, new_token_key_value, out_weight, kv_cache, lengths):
    f, t = lax.axis_index("fsdp"), lax.axis_index("tp")
    z_hi, x, core = f // 8, f // 2 % 4, f % 2
    z_lo = t // 4
    width = master.shape[1] // 8
    blocks = cast_blocks(master)

    def swap(piece):
        with jax.named_scope("core"):
            return send(piece, dc=1)

    def both(piece, z, hop, first=0):
        place_x = (x - hop) % 4
        return [(piece, first, z, place_x, core), (swap(piece), first, z, place_x, 1 - core)]

    def pick(value, index):
        return lax.dynamic_index_in_dim(value, index, 0, keepdims=False)

    with jax.named_scope("over_t"):
        own = lax.all_to_all(blocks, "tp", split_axis=0, concat_axis=0, tiled=True)
    r, s, w = queries.shape
    shares = attend(queries, new_token_key_value, kv_cache, out_weight, lengths, blocks)
    own, shares = fence(own, shares)

    with jax.named_scope("own_x"):
        own_1, own_3 = send(own, dx=1), send(own, dx=-1)
    with jax.named_scope("over_z"):
        dup = send(own, dz=2)
    with jax.named_scope("sum_y"):
        shares = lax.all_to_all(
            shares, "tp", split_axis=0, concat_axis=0, tiled=True,
            axis_index_groups=((0, 1, 2, 3), (4, 5, 6, 7)),
        )
    out = place(None, both(own, z_hi, 0))
    own_1, own_3, shares, out = fence(own_1, own_3, shares, out)

    low_1, high_3 = halves(own_1, own_3)
    with jax.named_scope("own_x2"):
        low_2, high_2 = send(low_1, dx=1), send(high_3, dx=-1)
    with jax.named_scope("dup_z"):
        dup_low_1 = send(low_1, dz=2)
    with jax.named_scope("dup_x"):
        dup_high_1, dup_3 = send(dup[4:], dx=1), send(dup, dx=-1)
        dup_high_1 = fence(dup_high_1, cost=1 << 20)
    out = place(out, both(own_1, z_hi, 1) + both(own_3, z_hi, 3))
    low_2, high_2, dup_low_1, shares, out = fence(low_2, high_2, dup_low_1, shares, out)

    with jax.named_scope("dup_x2"):
        dup_low_2 = send(dup_low_1, dx=1)
    with jax.named_scope("dup_z2"):
        dup_high_2 = send(high_2, dz=2)
    total = jnp.sum(shares, axis=0)
    kept, given = pick(total, z_lo), pick(total, 1 - z_lo)
    out = place(out, both(dup, 1 - z_hi, 0) + both(low_2, z_hi, 2) + both(high_2, z_hi, 2, 4)
        + both(dup_low_1, 1 - z_hi, 1))
    dup_high_1, dup_3, dup_low_2, dup_high_2, kept, given, out = fence(
        dup_high_1, dup_3, dup_low_2, dup_high_2, kept, given, out
    )

    with jax.named_scope("sum_z"):
        given = lax.ppermute(given, AXES, [(i, i ^ 4) for i in range(128)])
    pairs = [both(dup_high_1, 1 - z_hi, 1, 4), both(dup_3, 1 - z_hi, 3)]
    pairs += [both(dup_low_2, 1 - z_hi, 2), both(dup_high_2, 1 - z_hi, 2, 4)]
    out = place(out, [mine for mine, _ in pairs])
    out = place(out, [theirs for _, theirs in pairs])
    out, kept, given = fence(out, kept, given)
    attn = (kept + given).astype(jnp.bfloat16)
    return (out.reshape(-1, width), attn.reshape(r, s, -1))


def solution(mesh):
    in_specs = (
        P(("fsdp", "tp"), None),
        P("fsdp", None, "tp"),
        P("fsdp", None, None, "tp"),
        P("tp", None),
        P("fsdp", None, "tp", None, None),
        P("fsdp"),
    )
    out_specs = (P(None, "tp"), P("fsdp", None, "tp"))
    return jax.shard_map(local, mesh=mesh, in_specs=in_specs, out_specs=out_specs, check_vma=False)
```
